512 devices in a mesh: row: 32 (over z, y_hi, core), col: 16 (over x, y_lo).
Axes of the slice: x: 4, y: 8 (y_hi: 2, y_lo: 4; y = y_hi * 4 + y_lo), z: 8, core: 2. Of those that a mesh axis runs over, the one named last changes fastest.
Arguments:
- raw: bfloat16 [256, 4096, 512], P(None, ('row', 'col')), may hold values from -40 to 40
Outputs:
- stack: bfloat16 [2, 16, 4096, 4096], P(None, None, 'row', 'col')
The draws below stay inside these ranges and needn't reach their ends.
All inputs are finite; a program needn't handle non-finite values.
Results may differ from the reference program's by a relative error of at most 0.0054.
Values may be sent and summed in bfloat16 or wider, within the bound.
No kernel may reach another device: no remote copies, remote signals or barrier semaphores. Data moves between devices by JAX's collectives and lax.ppermute only.
A program may use at most 64 MiB of HBM per device.

```python
import jax
import jax.numpy as jnp
from jax import lax

CHANNELS = 4096
WINDOWS = 256
SAMPLES = 512
BINS = 16
LOW_BIN = 24
SPAN = 65
N_ROW = 32


def draw_raw(key, part):
    key = jax.random.fold_in(key, 11)
    key_noise, key_envelope = jax.random.split(key, 2)
    shape = (WINDOWS, CHANNELS, SAMPLES)
    segments = (WINDOWS, CHANNELS, SAMPLES // 32)
    noise = jnp.clip(jax.random.normal(key_noise, shape, jnp.float32), -4.0, 4.0)
    envelope = jnp.exp(jax.random.uniform(key_envelope, segments, jnp.float32, -1.5, 1.5))
    envelope = jnp.repeat(envelope, 32, axis=2)
    return jnp.clip(noise * envelope, -40.0, 40.0).astype(jnp.bfloat16)


def setup_inputs(seed: int = 0) -> dict:
    streams_of = jax.random.split(jax.random.key(seed), 2)
    return {
        "raw": draw_raw(jax.random.fold_in(streams_of[1], 71), 0),
    }


def running_band():
    steps = jnp.arange(SAMPLES)
    near = jnp.abs(steps[:, None] - steps[None, :]) <= SPAN // 2
    return near.astype(jnp.bfloat16)

def whiten_block(raw_block):
    count = raw_block.shape[1]
    flat = raw_block.reshape(-1, SAMPLES)
    magnitude = jnp.dot(jnp.abs(flat), running_band(), preferred_element_type=jnp.float32) / SPAN
    balanced = flat.astype(jnp.float32) / (magnitude + 1e-06)
    spectrum = jnp.fft.rfft(balanced, axis=-1)[:, LOW_BIN:LOW_BIN + BINS]
    spec_real = jnp.real(spectrum)
    spec_imag = jnp.imag(spectrum)
    energy = spec_real * spec_real + spec_imag * spec_imag
    level = lax.optimization_barrier(jnp.mean(energy, axis=1, keepdims=True))
    factor = lax.rsqrt(energy + 0.25 * level + 1.0)
    white_real = (spec_real * factor).astype(jnp.bfloat16).reshape(WINDOWS, count, BINS)
    white_imag = (spec_imag * factor).astype(jnp.bfloat16).reshape(WINDOWS, count, BINS)
    return (white_real, white_imag)

def reference(raw):
    block_size = CHANNELS // N_ROW
    nblocks = N_ROW
    blocks = raw.reshape(WINDOWS, nblocks, block_size, SAMPLES).transpose(1, 0, 2, 3)
    white_real, white_imag = lax.map(whiten_block, blocks)
    full_real = white_real.transpose(0, 2, 3, 1).reshape(CHANNELS, BINS, WINDOWS)
    full_imag = white_imag.transpose(0, 2, 3, 1).reshape(CHANNELS, BINS, WINDOWS)
    wide_real = full_real.astype(jnp.float32)
    wide_imag = full_imag.astype(jnp.float32)

    def stack_rows(pair):
        left_real = pair[0].astype(jnp.float32)
        left_imag = pair[1].astype(jnp.float32)
        cross_real = jnp.einsum('ibw,jbw->bij', left_real, wide_real) + jnp.einsum('ibw,jbw->bij', left_imag, wide_imag)
        cross_imag = jnp.einsum('ibw,jbw->bij', left_imag, wide_real) - jnp.einsum('ibw,jbw->bij', left_real, wide_imag)
        return (jnp.stack([cross_real, cross_imag]) / WINDOWS).astype(jnp.bfloat16)
    row_real = full_real.reshape(nblocks, block_size, BINS, WINDOWS)
    row_imag = full_imag.reshape(nblocks, block_size, BINS, WINDOWS)
    tiles = lax.map(stack_rows, (row_real, row_imag))
    return tiles.transpose(1, 2, 0, 3, 4).reshape(2, BINS, CHANNELS, CHANNELS)
```

```python
import math

import jax
import jax.numpy as jnp
import numpy as np
from jax import lax
from jax.experimental import pallas as pl
from jax.experimental.pallas import tpu as pltpu
from jax.sharding import Mesh, PartitionSpec as P

WINDOWS = 256
SAMPLES = 512
BINS = 16
LOW_BIN = 24
SPAN = 65
AXES = ("z", "yh", "core", "x", "yl")
SIZES = {"z": 8, "yh": 2, "core": 2, "x": 4, "yl": 4}
STEPS = 2
PER_STEP = WINDOWS // STEPS


def tables():
    steps = np.arange(SAMPLES)
    band = (np.abs(steps[:, None] - steps[None, :]) <= SPAN // 2).astype(np.float32)
    freqs = LOW_BIN + np.arange(BINS)
    angles = (steps[None, :] * freqs[:, None] % SAMPLES) * (2.0 * math.pi / SAMPLES)
    dft = np.concatenate([np.cos(angles), -np.sin(angles)], axis=0).astype(np.float32)
    high = dft.astype(jnp.bfloat16)
    low = (dft - high.astype(np.float32)).astype(jnp.bfloat16)
    return band.astype(jnp.bfloat16), np.concatenate([high, low], axis=0)


def nt_dot(left, right):
    return lax.dot_general(
        left, right, (((1,), (1,)), ((), ())), preferred_element_type=jnp.float32
    )


def whiten_kernel(raw_ref, band_ref, dft_ref, out_ref, balanced_ref, white_ref):
    flat = raw_ref[...]
    total = jnp.dot(jnp.abs(flat), band_ref[...], preferred_element_type=jnp.float32)
    balanced = flat.astype(jnp.float32) / (total * (1.0 / SPAN) + 1e-06)
    for part in range(4):
        balanced_ref[part] = balanced[:, part * 128 : (part + 1) * 128]
    dft = dft_ref[...]
    for channel in range(8):
        balanced = jnp.concatenate(
            [balanced_ref[part, pl.ds(channel, PER_STEP, stride=8), :] for part in range(4)],
            axis=1,
        )
        high = balanced.astype(jnp.bfloat16)
        low = (balanced - high.astype(jnp.float32)).astype(jnp.bfloat16)
        wide = nt_dot(dft, high)
        spectrum = wide[: 2 * BINS] + (wide[2 * BINS :] + nt_dot(dft[: 2 * BINS], low))
        real = spectrum[:BINS]
        imag = spectrum[BINS:]
        energy = real * real + imag * imag
        level = jnp.mean(energy, axis=0, keepdims=True)
        factor = lax.rsqrt(energy + 0.25 * level + 1.0)
        white_ref[:, channel, :PER_STEP] = real * factor
        white_ref[:, channel, PER_STEP:] = imag * factor
    out_ref[...] = white_ref[...].astype(jnp.bfloat16)


def whiten(raw):
    band, dft = tables()
    rows = PER_STEP * 8
    return pl.pallas_call(
        whiten_kernel,
        grid=(STEPS,),
        in_specs=[
            pl.BlockSpec((rows, SAMPLES), lambda g: (g, 0)),
            pl.BlockSpec((SAMPLES, SAMPLES), lambda g: (0, 0)),
            pl.BlockSpec((4 * BINS, SAMPLES), lambda g: (0, 0)),
        ],
        out_specs=pl.BlockSpec((BINS, 8, 2 * PER_STEP), lambda g: (0, 0, g)),
        out_shape=jax.ShapeDtypeStruct((BINS, 8, 2 * WINDOWS), jnp.bfloat16),
        scratch_shapes=[
            pltpu.VMEM((4, rows, 128), jnp.float32),
            pltpu.VMEM((BINS, 8, 2 * PER_STEP), jnp.float32),
        ],
        compiler_params=pltpu.CompilerParams(vmem_limit_bytes=32 << 20),
        cost_estimate=pl.CostEstimate(
            flops=3_000_000_000, bytes_accessed=3 << 20, transcendentals=1 << 20
        ),
        name="whiten",
    )(raw.reshape(WINDOWS * 8, SAMPLES), jnp.asarray(band), jnp.asarray(dft))


def cross_kernel(place_ref, rows_ref, *refs):
    pieces = refs[:8]
    out_ref, left_ref, right_ref, tile_ref, row_sem, piece_sem, out_sem = refs[8:]
    row_copy = pltpu.make_async_copy(rows_ref, left_ref, row_sem)
    row_copy.start()
    copies = []
    for piece in pieces:
        for slot in range(piece.shape[0]):
            k = len(copies)
            copy = pltpu.make_async_copy(
                piece.at[slot], right_ref.at[place_ref[k]], piece_sem.at[k]
            )
            copy.start()
            copies.append(copy)
    row_copy.wait()
    for copy in copies:
        copy.wait()
    half = PER_STEP
    outs = []
    for b in range(BINS):
        left = left_ref[:, b].astype(jnp.float32).reshape(128, 2 * WINDOWS)
        right = right_ref[:, b].astype(jnp.float32).reshape(256, 2 * WINDOWS)
        right = right.astype(jnp.bfloat16)
        turned = []
        for g in range(STEPS):
            turned.append(left[:, (2 * g + 1) * half : (2 * g + 2) * half])
            turned.append(-left[:, 2 * g * half : (2 * g + 1) * half])
        turned = jnp.concatenate(turned, axis=1).astype(jnp.bfloat16)
        left = left.astype(jnp.bfloat16)
        tile_ref[0, b] = (nt_dot(left, right) * (1.0 / WINDOWS)).astype(jnp.bfloat16)
        tile_ref[1, b] = (nt_dot(turned, right) * (1.0 / WINDOWS)).astype(jnp.bfloat16)
        if b % 4 == 3:
            part = pl.ds(b - 3, 4)
            copy = pltpu.make_async_copy(
                tile_ref.at[:, part], out_ref.at[:, part], out_sem.at[b // 4]
            )
            copy.start()
            outs.append(copy)
    for copy in outs:
        copy.wait()


def cross(places, rows, pieces):
    block = (BINS, 8, 2 * WINDOWS)
    out = (2, BINS, 128, 256)
    anywhere = pl.BlockSpec(memory_space=pl.ANY)
    return pl.pallas_call(
        cross_kernel,
        in_specs=[pl.BlockSpec(memory_space=pltpu.SMEM)] + [anywhere] * 9,
        out_specs=anywhere,
        out_shape=jax.ShapeDtypeStruct(out, jnp.bfloat16),
        scratch_shapes=[
            pltpu.VMEM((16,) + block, jnp.bfloat16),
            pltpu.VMEM((32,) + block, jnp.bfloat16),
            pltpu.VMEM(out, jnp.bfloat16),
            pltpu.SemaphoreType.DMA,
            pltpu.SemaphoreType.DMA((32,)),
            pltpu.SemaphoreType.DMA((4,)),
        ],
        compiler_params=pltpu.CompilerParams(vmem_limit_bytes=48 << 20),
        cost_estimate=pl.CostEstimate(
            flops=1_100_000_000, bytes_accessed=8 << 20, transcendentals=0
        ),
        name="cross",
    )(places, rows, *pieces)


def flat(z, yh, core, x, yl):
    return (((z * 2 + yh) * 2 + core) * 4 + x) * 4 + yl


def everyone():
    for index in np.ndindex(*(SIZES[a] for a in AXES)):
        yield index


def spread_pairs(turn):
    pairs = []
    for z, yh, core, x, yl in everyone():
        home = z * 2 + yh
        target = (turn + x) % 4
        layer = (x + yl + z) % 4 + 4 * (target // 2)
        pairs.append((flat(z, yh, core, x, yl), flat(layer, target % 2, core, home // 4, home % 4)))
    return pairs


def ring(value, axis, by):
    n = SIZES[axis]
    return lax.ppermute(value, axis, [(i, (i + by) % n) for i in range(n)])


def swap(value):
    return ring(value, "core", 1)


def places_here():
    table = []
    for z, yh, core, x, yl in everyone():
        home_z = (x * 4 + yl) // 2
        row = []
        for side in (core, 1 - core):
            for away, slots in ((0, 4), (-1, 4), (1, 4), (-2, 2), (2, 2)):
                layer = (z + away) % 8
                for slot in range(slots):
                    from_x = (2 * (layer // 4) + yh - slot) % 4
                    row.append(side * 16 + from_x * 4 + (layer - from_x - home_z) % 4)
        assert sorted(row) == list(range(32))
        table.append(row)
    table = jnp.asarray(np.array(table, np.int32))
    return lax.dynamic_index_in_dim(table, lax.axis_index(AXES), keepdims=False)


def on_device(raw):
    white = whiten(raw)
    here = jnp.stack([lax.ppermute(white, AXES, spread_pairs(turn)) for turn in range(4)])
    rows = lax.all_gather(lax.all_gather(white, "yl"), "x")
    rows = rows.reshape((16,) + white.shape)
    below = ring(here, "z", 1)
    above = ring(here, "z", -1)
    far = jnp.concatenate([ring(below[:2], "z", 1), ring(above[:2], "z", -1)])
    mine = [here, below, above, far]
    pieces = mine + [swap(piece) for piece in mine]
    return cross(places_here(), rows, pieces)


def solution(mesh):
    split = Mesh(mesh.devices.reshape([SIZES[a] for a in AXES]), AXES)
    return jax.shard_map(
        on_device,
        mesh=split,
        in_specs=(P(None, AXES, None),),
        out_specs=P(None, None, ("z", "yh", "core"), ("x", "yl")),
        check_vma=False,
    )
```

```python
import math

import jax
import jax.numpy as jnp
import numpy as np
from jax import lax
from jax.experimental import pallas as pl
from jax.experimental.pallas import tpu as pltpu
from jax.sharding import Mesh, PartitionSpec as P

WINDOWS = 256
SAMPLES = 512
BINS = 16
LOW_BIN = 24
SPAN = 65
AXES = ("z", "yh", "core", "x", "yl")
SIZES = {"z": 8, "yh": 2, "core": 2, "x": 4, "yl": 4}
CHUNKS = 4
CHUNK = WINDOWS // CHUNKS
HALF = WINDOWS // 2


def dft_table():
    steps = np.arange(SAMPLES)
    freqs = LOW_BIN + np.arange(BINS)
    angles = (steps[None, :] * freqs[:, None] % SAMPLES) * (2.0 * math.pi / SAMPLES)
    dft = np.concatenate([np.cos(angles), -np.sin(angles)], axis=0).astype(np.float32)
    high = dft.astype(jnp.bfloat16)
    low = (dft - high.astype(np.float32)).astype(jnp.bfloat16)
    return np.concatenate([high, low], axis=0)


def nt_dot(left, right):
    return lax.dot_general(
        left, right, (((1,), (1,)), ((), ())), preferred_element_type=jnp.float32
    )


def whiten_kernel(raw_ref, dft_ref, out_ref, chunk_ref, table_ref, balanced_ref, white_ref, sems):
    rows = CHUNK * 8
    copies = [
        pltpu.make_async_copy(
            raw_ref.at[pl.ds(chunk * rows, rows)], chunk_ref.at[chunk], sems.at[chunk]
        )
        for chunk in range(CHUNKS)
    ]
    for copy in copies:
        copy.start()
    table_copy = pltpu.make_async_copy(dft_ref, table_ref, sems.at[CHUNKS])
    table_copy.start()
    here = lax.broadcasted_iota(jnp.int32, (SAMPLES, SAMPLES), 0)
    there = lax.broadcasted_iota(jnp.int32, (SAMPLES, SAMPLES), 1)
    near = jnp.abs(here - there) <= SPAN // 2
    band = jnp.where(near, 1.0, 0.0).astype(jnp.bfloat16)
    table_copy.wait()
    dft = table_ref[...]
    per_half = CHUNKS // 2
    for half in range(2):
        for part in range(per_half):
            chunk = half * per_half + part
            copies[chunk].wait()
            flat = chunk_ref[chunk]
            total = jnp.dot(jnp.abs(flat), band, preferred_element_type=jnp.float32)
            balanced = flat.astype(jnp.float32) / (total * (1.0 / SPAN) + 1e-06)
            for lane in range(4):
                balanced_ref[lane, pl.ds(chunk * rows, rows), :] = balanced[
                    :, lane * 128 : (lane + 1) * 128
                ]
        first = half * HALF * 8
        for channel in range(8):
            balanced = jnp.concatenate(
                [
                    balanced_ref[lane, pl.ds(first + channel, HALF, stride=8), :]
                    for lane in range(4)
                ],
                axis=1,
            )
            high = balanced.astype(jnp.bfloat16)
            low = (balanced - high.astype(jnp.float32)).astype(jnp.bfloat16)
            wide = nt_dot(dft, high)
            spectrum = wide[: 2 * BINS] + (wide[2 * BINS :] + nt_dot(dft[: 2 * BINS], low))
            real = spectrum[:BINS]
            imag = spectrum[BINS:]
            energy = real * real + imag * imag
            level = jnp.mean(energy, axis=0, keepdims=True)
            factor = lax.rsqrt(energy + 0.25 * level + 1.0)
            at = half * HALF
            white_ref[:, channel, at : at + HALF] = real * factor
            white_ref[:, channel, WINDOWS + at : WINDOWS + at + HALF] = imag * factor
    out_ref[...] = white_ref[...].astype(jnp.bfloat16)


def whiten(raw):
    anywhere = pl.BlockSpec(memory_space=pl.ANY)
    return pl.pallas_call(
        whiten_kernel,
        in_specs=[anywhere, anywhere],
        out_specs=pl.BlockSpec(memory_space=pltpu.VMEM),
        out_shape=jax.ShapeDtypeStruct((BINS, 8, 2 * WINDOWS), jnp.bfloat16),
        scratch_shapes=[
            pltpu.VMEM((CHUNKS, CHUNK * 8, SAMPLES), jnp.bfloat16),
            pltpu.VMEM((4 * BINS, SAMPLES), jnp.bfloat16),
            pltpu.VMEM((4, WINDOWS * 8, 128), jnp.float32),
            pltpu.VMEM((BINS, 8, 2 * WINDOWS), jnp.float32),
            pltpu.SemaphoreType.DMA((CHUNKS + 1,)),
        ],
        compiler_params=pltpu.CompilerParams(vmem_limit_bytes=60 << 20),
        cost_estimate=pl.CostEstimate(
            flops=3_000_000_000, bytes_accessed=3 << 20, transcendentals=1 << 20
        ),
        name="whiten",
    )(raw.reshape(WINDOWS * 8, SAMPLES), jnp.asarray(dft_table()))


def cross_kernel(place_ref, rows_ref, *refs):
    pieces = refs[:8]
    out_ref, left_ref, right_ref, tile_ref, row_sem, out_sem = refs[8:]
    row_copies = [
        pltpu.make_async_copy(rows_ref.at[k], left_ref.at[place_ref[32 + k]], row_sem.at[k])
        for k in range(16)
    ]
    for copy in row_copies:
        copy.start()

    def gather(b):
        k = 0
        for piece in pieces:
            for slot in range(piece.shape[0]):
                right_ref[b, place_ref[k]] = piece[slot, b]
                k += 1

    gather(0)
    for copy in row_copies:
        copy.wait()
    outs = []
    for b in range(BINS):
        if b + 1 < BINS:
            gather(b + 1)
        left = left_ref[:, b].reshape(128, 2 * WINDOWS)
        right = right_ref[b].reshape(256, 2 * WINDOWS)
        turned = jnp.concatenate([left[:, WINDOWS:], -left[:, :WINDOWS]], axis=1)
        both = jnp.concatenate([left, turned], axis=0)
        tile = (nt_dot(both, right) * (1.0 / WINDOWS)).astype(jnp.bfloat16)
        tile_ref[0, b] = tile[:128]
        tile_ref[1, b] = tile[128:]
        if b % 4 == 3:
            part = pl.ds(b - 3, 4)
            copy = pltpu.make_async_copy(
                tile_ref.at[:, part], out_ref.at[:, part], out_sem.at[b // 4]
            )
            copy.start()
            outs.append(copy)
    for copy in outs:
        copy.wait()


def cross(places, rows, pieces):
    block = (BINS, 8, 2 * WINDOWS)
    out = (2, BINS, 128, 256)
    anywhere = pl.BlockSpec(memory_space=pl.ANY)
    return pl.pallas_call(
        cross_kernel,
        in_specs=[pl.BlockSpec(memory_space=pltpu.SMEM), pl.BlockSpec(memory_space=pltpu.HBM)]
        + [pl.BlockSpec(memory_space=pltpu.VMEM)] * 8,
        out_specs=anywhere,
        out_shape=jax.ShapeDtypeStruct(out, jnp.bfloat16),
        scratch_shapes=[
            pltpu.VMEM((16,) + block, jnp.bfloat16),
            pltpu.VMEM((BINS, 32, 8, 2 * WINDOWS), jnp.bfloat16),
            pltpu.VMEM(out, jnp.bfloat16),
            pltpu.SemaphoreType.DMA((16,)),
            pltpu.SemaphoreType.DMA((4,)),
        ],
        compiler_params=pltpu.CompilerParams(vmem_limit_bytes=40 << 20),
        cost_estimate=pl.CostEstimate(
            flops=1_100_000_000, bytes_accessed=8 << 20, transcendentals=0
        ),
        name="cross",
    )(places, rows, *pieces)


def flat(z, yh, core, x, yl):
    return (((z * 2 + yh) * 2 + core) * 4 + x) * 4 + yl


def everyone():
    for index in np.ndindex(*(SIZES[a] for a in AXES)):
        yield index


def spread_pairs(turn):
    pairs = []
    for z, yh, core, x, yl in everyone():
        home = z * 2 + yh
        target = (turn + x) % 4
        layer = (x + yl + z) % 4 + 4 * (target // 2)
        pairs.append((flat(z, yh, core, x, yl), flat(layer, target % 2, core, home // 4, home % 4)))
    return pairs


def ring(value, axis, by):
    n = SIZES[axis]
    return lax.ppermute(value, axis, [(i, (i + by) % n) for i in range(n)])


def swap(value):
    return ring(value, "core", 1)


def places_here():
    table = []
    for z, yh, core, x, yl in everyone():
        home_z = (x * 4 + yl) // 2
        row = []
        for side in (core, 1 - core):
            for away, slots in ((0, 4), (-1, 4), (1, 4), (-2, 2), (2, 2)):
                layer = (z + away) % 8
                for slot in range(slots):
                    from_x = (2 * (layer // 4) + yh - slot) % 4
                    row.append(side * 16 + from_x * 4 + (layer - from_x - home_z) % 4)
        assert sorted(row) == list(range(32))
        row.extend(k // 4 * 4 + (yl - k % 4) % 4 for k in range(16))
        table.append(row)
    table = jnp.asarray(np.array(table, np.int32))
    return lax.dynamic_index_in_dim(table, lax.axis_index(AXES), keepdims=False)


def on_device(raw):
    white = whiten(raw)
    here = jnp.stack([lax.ppermute(white, AXES, spread_pairs(turn)) for turn in range(4)])
    near = jnp.stack([white] + [ring(white, "yl", by) for by in (1, 2, 3)])
    rows = lax.all_gather(near, "x").reshape((16,) + white.shape)
    below = ring(here, "z", 1)
    above = ring(here, "z", -1)
    far = jnp.concatenate([ring(below[:2], "z", 1), ring(above[:2], "z", -1)])
    mine = [here, below, above, far]
    pieces = mine + [swap(piece) for piece in mine]
    return cross(places_here(), rows, pieces)


def solution(mesh):
    split = Mesh(mesh.devices.reshape([SIZES[a] for a in AXES]), AXES)
    return jax.shard_map(
        on_device,
        mesh=split,
        in_specs=(P(None, AXES, None),),
        out_specs=P(None, None, ("z", "yh", "core"), ("x", "yl")),
        check_vma=False,
    )
```

```python
import itertools
import math

import jax
import jax.numpy as jnp
import numpy as np
from jax import lax
from jax.experimental import pallas as pl
from jax.experimental.pallas import tpu as pltpu
from jax.sharding import Mesh, PartitionSpec as P

WINDOWS = 256
SAMPLES = 512
BINS = 16
LOW_BIN = 24
SPAN = 65
AXES = ("z", "yh", "core", "x", "yl")
SIZES = {"z": 8, "yh": 2, "core": 2, "x": 4, "yl": 4}
CHUNKS = 4
CHUNK = WINDOWS // CHUNKS
HALF = WINDOWS // 2
GROUP = 4


def dft_table():
    steps = np.arange(SAMPLES)
    freqs = LOW_BIN + np.arange(BINS)
    angles = (steps[None, :] * freqs[:, None] % SAMPLES) * (2.0 * math.pi / SAMPLES)
    dft = np.concatenate([np.cos(angles), -np.sin(angles)], axis=0).astype(np.float32)
    high = dft.astype(jnp.bfloat16)
    low = (dft - high.astype(np.float32)).astype(jnp.bfloat16)
    return np.concatenate([high, low], axis=0)


def nt_dot(left, right):
    return lax.dot_general(
        left, right, (((1,), (1,)), ((), ())), preferred_element_type=jnp.float32
    )


def whiten_kernel(raw_ref, dft_ref, out_ref, chunk_ref, table_ref, balanced_ref, white_ref, sems):
    rows = CHUNK * 8
    copies = [
        pltpu.make_async_copy(
            raw_ref.at[pl.ds(chunk * rows, rows)], chunk_ref.at[chunk], sems.at[chunk]
        )
        for chunk in range(CHUNKS)
    ]
    for copy in copies:
        copy.start()
    table_copy = pltpu.make_async_copy(dft_ref, table_ref, sems.at[CHUNKS])
    table_copy.start()
    here = lax.broadcasted_iota(jnp.int32, (SAMPLES, SAMPLES), 0)
    there = lax.broadcasted_iota(jnp.int32, (SAMPLES, SAMPLES), 1)
    near = jnp.abs(here - there) <= SPAN // 2
    band = jnp.where(near, 1.0, 0.0).astype(jnp.bfloat16)
    table_copy.wait()
    dft = table_ref[...]
    per_half = CHUNKS // 2
    for half in range(2):
        for part in range(per_half):
            chunk = half * per_half + part
            copies[chunk].wait()
            flat = chunk_ref[chunk]
            total = jnp.dot(jnp.abs(flat), band, preferred_element_type=jnp.float32)
            balanced = flat.astype(jnp.float32) / (total * (1.0 / SPAN) + 1e-06)
            for lane in range(4):
                balanced_ref[lane, pl.ds(chunk * rows, rows), :] = balanced[
                    :, lane * 128 : (lane + 1) * 128
                ]
        first = half * HALF * 8
        for channel in range(8):
            balanced = jnp.concatenate(
                [
                    balanced_ref[lane, pl.ds(first + channel, HALF, stride=8), :]
                    for lane in range(4)
                ],
                axis=1,
            )
            high = balanced.astype(jnp.bfloat16)
            low = (balanced - high.astype(jnp.float32)).astype(jnp.bfloat16)
            wide = nt_dot(dft, high)
            spectrum = wide[: 2 * BINS] + (wide[2 * BINS :] + nt_dot(dft[: 2 * BINS], low))
            real = spectrum[:BINS]
            imag = spectrum[BINS:]
            energy = real * real + imag * imag
            level = jnp.mean(energy, axis=0, keepdims=True)
            factor = lax.rsqrt(energy + 0.25 * level + 1.0)
            at = half * HALF
            white_ref[:, channel, at : at + HALF] = real * factor
            white_ref[:, channel, WINDOWS + at : WINDOWS + at + HALF] = imag * factor
    out_ref[...] = white_ref[...].astype(jnp.bfloat16)


def whiten(raw):
    anywhere = pl.BlockSpec(memory_space=pl.ANY)
    return pl.pallas_call(
        whiten_kernel,
        in_specs=[anywhere, anywhere],
        out_specs=pl.BlockSpec(memory_space=pltpu.VMEM),
        out_shape=jax.ShapeDtypeStruct((BINS, 8, 2 * WINDOWS), jnp.bfloat16),
        scratch_shapes=[
            pltpu.VMEM((CHUNKS, CHUNK * 8, SAMPLES), jnp.bfloat16),
            pltpu.VMEM((4 * BINS, SAMPLES), jnp.bfloat16),
            pltpu.VMEM((4, WINDOWS * 8, 128), jnp.float32),
            pltpu.VMEM((BINS, 8, 2 * WINDOWS), jnp.float32),
            pltpu.SemaphoreType.DMA((CHUNKS + 1,)),
        ],
        compiler_params=pltpu.CompilerParams(vmem_limit_bytes=60 << 20),
        cost_estimate=pl.CostEstimate(
            flops=3_000_000_000, bytes_accessed=3 << 20, transcendentals=1 << 20
        ),
        name="whiten",
    )(raw.reshape(WINDOWS * 8, SAMPLES), jnp.asarray(dft_table()))


def multiply(left, right):
    turned = jnp.concatenate([left[:, WINDOWS:], -left[:, :WINDOWS]], axis=1)
    both = jnp.concatenate([left, turned], axis=0)
    tile = (nt_dot(both, right) * (1.0 / WINDOWS)).astype(jnp.bfloat16)
    return tile[:128], tile[128:]


def cross_kernel(place_ref, *refs):
    count = len(refs) - 5
    pieces = refs[:count]
    out_ref, left_ref, right_ref, tile_ref, out_sem = refs[count:]

    def gather(b):
        for k, piece in enumerate(pieces):
            target = left_ref if k < 4 else right_ref
            target[b, place_ref[k]] = piece[:, b]

    gather(0)
    outs = []
    for b in range(BINS):
        if b + 1 < BINS:
            gather(b + 1)
        left = left_ref[b].reshape(128, 2 * WINDOWS)
        right = right_ref[b].reshape(256, 2 * WINDOWS)
        tile_ref[0, b], tile_ref[1, b] = multiply(left, right)
        if b % GROUP == GROUP - 1:
            bins = pl.ds(b - GROUP + 1, GROUP)
            copy = pltpu.make_async_copy(
                tile_ref.at[:, bins], out_ref.at[:, bins], out_sem.at[b // GROUP]
            )
            copy.start()
            outs.append(copy)
    for copy in outs:
        copy.wait()


def cross(places, pieces):
    out = (2, BINS, 128, 256)
    return pl.pallas_call(
        cross_kernel,
        in_specs=[pl.BlockSpec(memory_space=pltpu.SMEM)]
        + [pl.BlockSpec(memory_space=pltpu.VMEM)] * len(pieces),
        out_specs=pl.BlockSpec(memory_space=pl.ANY),
        out_shape=jax.ShapeDtypeStruct(out, jnp.bfloat16),
        scratch_shapes=[
            pltpu.VMEM((BINS, 4, 4, 8, 2 * WINDOWS), jnp.bfloat16),
            pltpu.VMEM((BINS, 8, 4, 8, 2 * WINDOWS), jnp.bfloat16),
            pltpu.VMEM(out, jnp.bfloat16),
            pltpu.SemaphoreType.DMA((BINS // GROUP,)),
        ],
        compiler_params=pltpu.CompilerParams(vmem_limit_bytes=40 << 20),
        cost_estimate=pl.CostEstimate(
            flops=1_100_000_000, bytes_accessed=8 << 20, transcendentals=0
        ),
        name="cross",
    )(places, *pieces)


def flat(z, yh, core, x, yl):
    return (((z * 2 + yh) * 2 + core) * 4 + x) * 4 + yl


def everyone():
    for index in np.ndindex(*(SIZES[a] for a in AXES)):
        yield index


def layer_class(z, x):
    return (x + z + z // 2) % 4


def ring_distance(a, b):
    return min((a - b) % 8, (b - a) % 8)


def spread_pairs():
    pairs = []
    for z, yh, x in np.ndindex(8, 2, 4):
        home = z * 2 + yh
        layer = layer_class(z, x)
        wanted = [(layer + 4 * up, half) for up in range(2) for half in range(2)]

        def way(order):
            return sum(
                ring_distance(4 * yh + yl, 4 * half + home % 4)
                for yl, (_, half) in enumerate(order)
            )

        order = min(itertools.permutations(wanted), key=way)
        for yl, (to_z, half) in enumerate(order):
            for core in range(2):
                pairs.append(
                    (flat(z, yh, core, x, yl), flat(to_z, half, core, home // 4, home % 4))
                )
    return pairs


def ring(value, axis, by):
    n = SIZES[axis]
    return lax.ppermute(value, axis, [(i, (i + by) % n) for i in range(n)])


def swap(value):
    return ring(value, "core", 1)


def places_here():
    table = []
    for z, yh, core, x, yl in everyone():
        rows = [(x + away) % 4 for away in (0, -1, 1, 2)]
        cols = []
        home_z = (x * 4 + yl) // 2
        for side in (core, 1 - core):
            for away in (0, -1, 1, 2):
                layer = (z + away) % 8
                (from_x,) = (k for k in range(4) if layer_class(home_z, k) == layer % 4)
                cols.append(side * 4 + from_x)
        assert sorted(rows) == list(range(4)) and sorted(cols) == list(range(8))
        table.append(rows + cols)
    table = jnp.asarray(np.array(table, np.int32))
    return lax.dynamic_index_in_dim(table, lax.axis_index(AXES), keepdims=False)


def on_device(raw):
    white = whiten(raw)
    near = lax.all_gather(white, "yl")
    here = lax.ppermute(near, AXES, spread_pairs())
    rows = [near] + [ring(near, "x", by) for by in (1, -1, 2)]
    below = ring(here, "z", 1)
    above = ring(here, "z", -1)
    far = jnp.concatenate([ring(below[:2], "z", 1), ring(above[2:], "z", -1)])
    mine = [here, below, above, far]
    pieces = rows + mine + [swap(piece) for piece in mine]
    return cross(places_here(), pieces)


def solution(mesh):
    split = Mesh(mesh.devices.reshape([SIZES[a] for a in AXES]), AXES)
    return jax.shard_map(
        on_device,
        mesh=split,
        in_specs=(P(None, AXES, None),),
        out_specs=P(None, None, ("z", "yh", "core"), ("x", "yl")),
        check_vma=False,
    )
```

```python
import itertools
import math

import jax
import jax.numpy as jnp
import numpy as np
from jax import lax
from jax.experimental import pallas as pl
from jax.experimental.pallas import tpu as pltpu
from jax.sharding import Mesh, PartitionSpec as P

WINDOWS = 256
SAMPLES = 512
BINS = 16
LOW_BIN = 24
SPAN = 65
AXES = ("z", "yh", "core", "x", "yl")
SIZES = {"z": 8, "yh": 2, "core": 2, "x": 4, "yl": 4}
CHUNKS = 4
CHUNK = WINDOWS // CHUNKS
HALF = WINDOWS // 2
GROUP = 4


def dft_table():
    steps = np.arange(SAMPLES)
    freqs = LOW_BIN + np.arange(BINS)
    angles = (steps[None, :] * freqs[:, None] % SAMPLES) * (2.0 * math.pi / SAMPLES)
    dft = np.concatenate([np.cos(angles), -np.sin(angles)], axis=0).astype(np.float32)
    high = dft.astype(jnp.bfloat16)
    low = (dft - high.astype(np.float32)).astype(jnp.bfloat16)
    return np.concatenate([high, low], axis=0)


def nt_dot(left, right):
    return lax.dot_general(
        left, right, (((1,), (1,)), ((), ())), preferred_element_type=jnp.float32
    )


def whiten_kernel(raw_ref, dft_ref, out_ref, chunk_ref, table_ref, balanced_ref, white_ref, sems):
    rows = CHUNK * 8
    copies = [
        pltpu.make_async_copy(
            raw_ref.at[pl.ds(chunk * rows, rows)], chunk_ref.at[chunk], sems.at[chunk]
        )
        for chunk in range(CHUNKS)
    ]
    for copy in copies:
        copy.start()
    table_copy = pltpu.make_async_copy(dft_ref, table_ref, sems.at[CHUNKS])
    table_copy.start()
    here = lax.broadcasted_iota(jnp.int32, (SAMPLES, SAMPLES), 0)
    there = lax.broadcasted_iota(jnp.int32, (SAMPLES, SAMPLES), 1)
    near = jnp.abs(here - there) <= SPAN // 2
    band = jnp.where(near, 1.0, 0.0).astype(jnp.bfloat16)
    table_copy.wait()
    dft = table_ref[...]
    per_half = CHUNKS // 2
    for half in range(2):
        for part in range(per_half):
            chunk = half * per_half + part
            copies[chunk].wait()
            flat = chunk_ref[chunk]
            total = jnp.dot(jnp.abs(flat), band, preferred_element_type=jnp.float32)
            balanced = flat.astype(jnp.float32) / (total * (1.0 / SPAN) + 1e-06)
            for lane in range(4):
                balanced_ref[lane, pl.ds(chunk * rows, rows), :] = balanced[
                    :, lane * 128 : (lane + 1) * 128
                ]
        first = half * HALF * 8
        for channel in range(8):
            balanced = jnp.concatenate(
                [
                    balanced_ref[lane, pl.ds(first + channel, HALF, stride=8), :]
                    for lane in range(4)
                ],
                axis=1,
            )
            high = balanced.astype(jnp.bfloat16)
            low = (balanced - high.astype(jnp.float32)).astype(jnp.bfloat16)
            wide = nt_dot(dft, high)
            spectrum = wide[: 2 * BINS] + (wide[2 * BINS :] + nt_dot(dft[: 2 * BINS], low))
            real = spectrum[:BINS]
            imag = spectrum[BINS:]
            energy = real * real + imag * imag
            level = jnp.mean(energy, axis=0, keepdims=True)
            factor = lax.rsqrt(energy + 0.25 * level + 1.0)
            at = half * HALF
            white_ref[:, channel, at : at + HALF] = real * factor
            white_ref[:, channel, WINDOWS + at : WINDOWS + at + HALF] = imag * factor
    out_ref[...] = white_ref[...].astype(jnp.bfloat16)


def whiten(raw):
    anywhere = pl.BlockSpec(memory_space=pl.ANY)
    return pl.pallas_call(
        whiten_kernel,
        in_specs=[anywhere, anywhere],
        out_specs=pl.BlockSpec(memory_space=pltpu.VMEM),
        out_shape=jax.ShapeDtypeStruct((BINS, 8, 2 * WINDOWS), jnp.bfloat16),
        scratch_shapes=[
            pltpu.VMEM((CHUNKS, CHUNK * 8, SAMPLES), jnp.bfloat16),
            pltpu.VMEM((4 * BINS, SAMPLES), jnp.bfloat16),
            pltpu.VMEM((4, WINDOWS * 8, 128), jnp.float32),
            pltpu.VMEM((BINS, 8, 2 * WINDOWS), jnp.float32),
            pltpu.SemaphoreType.DMA((CHUNKS + 1,)),
        ],
        compiler_params=pltpu.CompilerParams(vmem_limit_bytes=60 << 20),
        cost_estimate=pl.CostEstimate(
            flops=3_000_000_000, bytes_accessed=3 << 20, transcendentals=1 << 20
        ),
        name="whiten",
    )(raw.reshape(WINDOWS * 8, SAMPLES), jnp.asarray(dft_table()))


def multiply(left, right):
    turned = jnp.concatenate([left[:, WINDOWS:], -left[:, :WINDOWS]], axis=1)
    both = jnp.concatenate([left, turned], axis=0)
    tile = (nt_dot(both, right) * (1.0 / WINDOWS)).astype(jnp.bfloat16)
    return tile[:128], tile[128:]


def cross_kernel(place_ref, *refs):
    count = len(refs) - 5
    pieces = refs[:count]
    out_ref, left_ref, right_ref, tile_ref, out_sem = refs[count:]

    def gather(b):
        for k in range(4):
            left_ref[b, k] = pieces[0][4 * k : 4 * k + 4, b]
        for k, piece in enumerate(pieces[1:]):
            right_ref[b, place_ref[4 + k]] = piece[:, b]

    gather(0)
    outs = []
    for b in range(BINS):
        if b + 1 < BINS:
            gather(b + 1)
        left = left_ref[b].reshape(128, 2 * WINDOWS)
        right = right_ref[b].reshape(256, 2 * WINDOWS)
        tile_ref[0, b], tile_ref[1, b] = multiply(left, right)
        if b % GROUP == GROUP - 1:
            bins = pl.ds(b - GROUP + 1, GROUP)
            copy = pltpu.make_async_copy(
                tile_ref.at[:, bins], out_ref.at[:, bins], out_sem.at[b // GROUP]
            )
            copy.start()
            outs.append(copy)
    for copy in outs:
        copy.wait()


def cross(places, pieces):
    out = (2, BINS, 128, 256)
    return pl.pallas_call(
        cross_kernel,
        in_specs=[pl.BlockSpec(memory_space=pltpu.SMEM)]
        + [pl.BlockSpec(memory_space=pltpu.VMEM)] * len(pieces),
        out_specs=pl.BlockSpec(memory_space=pl.ANY),
        out_shape=jax.ShapeDtypeStruct(out, jnp.bfloat16),
        scratch_shapes=[
            pltpu.VMEM((BINS, 4, 4, 8, 2 * WINDOWS), jnp.bfloat16),
            pltpu.VMEM((BINS, 8, 4, 8, 2 * WINDOWS), jnp.bfloat16),
            pltpu.VMEM(out, jnp.bfloat16),
            pltpu.SemaphoreType.DMA((BINS // GROUP,)),
        ],
        compiler_params=pltpu.CompilerParams(vmem_limit_bytes=40 << 20),
        cost_estimate=pl.CostEstimate(
            flops=1_100_000_000, bytes_accessed=8 << 20, transcendentals=0
        ),
        name="cross",
    )(places, *pieces)


def flat(z, yh, core, x, yl):
    return (((z * 2 + yh) * 2 + core) * 4 + x) * 4 + yl


def everyone():
    for index in np.ndindex(*(SIZES[a] for a in AXES)):
        yield index


def layer_class(z, x):
    return (x + z + z // 2) % 4


def ring_distance(a, b):
    return min((a - b) % 8, (b - a) % 8)


def spread_pairs():
    pairs = []
    for z, yh, x in np.ndindex(8, 2, 4):
        home = z * 2 + yh
        layer = layer_class(z, x)
        wanted = [(layer + 4 * up, half) for up in range(2) for half in range(2)]

        def way(order):
            return sum(
                ring_distance(4 * yh + yl, 4 * half + home % 4)
                for yl, (_, half) in enumerate(order)
            )

        order = min(itertools.permutations(wanted), key=way)
        for yl, (to_z, half) in enumerate(order):
            for core in range(2):
                pairs.append(
                    (flat(z, yh, core, x, yl), flat(to_z, half, core, home // 4, home % 4))
                )
    return pairs


def ring(value, axis, by):
    n = SIZES[axis]
    return lax.ppermute(value, axis, [(i, (i + by) % n) for i in range(n)])


def swap(value):
    return ring(value, "core", 1)


def places_here():
    table = []
    for z, yh, core, x, yl in everyone():
        rows = [(x + away) % 4 for away in (0, -1, 1, 2)]
        cols = []
        home_z = (x * 4 + yl) // 2
        for side in (core, 1 - core):
            for away in (0, -1, 1, 2):
                layer = (z + away) % 8
                (from_x,) = (k for k in range(4) if layer_class(home_z, k) == layer % 4)
                cols.append(side * 4 + from_x)
        assert sorted(rows) == list(range(4)) and sorted(cols) == list(range(8))
        table.append(rows + cols)
    table = jnp.asarray(np.array(table, np.int32))
    return lax.dynamic_index_in_dim(table, lax.axis_index(AXES), keepdims=False)


def on_device(raw):
    white = whiten(raw)
    near = lax.all_gather(white, "yl")
    here = lax.ppermute(near, AXES, spread_pairs())
    rows = lax.all_to_all(jnp.broadcast_to(near[None], (4,) + near.shape), "x", 0, 0)
    rows = [rows.reshape((16,) + white.shape)]
    below = ring(here, "z", 1)
    above = ring(here, "z", -1)
    far = jnp.concatenate([ring(below[:2], "z", 1), ring(above[2:], "z", -1)])
    mine = [here, below, above, far]
    pieces = rows + mine + [swap(piece) for piece in mine]
    return cross(places_here(), pieces)


def solution(mesh):
    split = Mesh(mesh.devices.reshape([SIZES[a] for a in AXES]), AXES)
    return jax.shard_map(
        on_device,
        mesh=split,
        in_specs=(P(None, AXES, None),),
        out_specs=P(None, None, ("z", "yh", "core"), ("x", "yl")),
        check_vma=False,
    )
```

```python
import itertools
import math

import jax
import jax.numpy as jnp
import numpy as np
from jax import lax
from jax.experimental import pallas as pl
from jax.experimental.pallas import tpu as pltpu
from jax.sharding import Mesh, PartitionSpec as P

WINDOWS = 256
SAMPLES = 512
BINS = 16
LOW_BIN = 24
SPAN = 65
AXES = ("z", "yh", "core", "x", "yl")
SIZES = {"z": 8, "yh": 2, "core": 2, "x": 4, "yl": 4}
CHUNKS = 4
CHUNK = WINDOWS // CHUNKS
HALF = WINDOWS // 2
GROUP = 4


def dft_table():
    steps = np.arange(SAMPLES)
    freqs = LOW_BIN + np.arange(BINS)
    angles = (steps[None, :] * freqs[:, None] % SAMPLES) * (2.0 * math.pi / SAMPLES)
    dft = np.concatenate([np.cos(angles), -np.sin(angles)], axis=0).astype(np.float32)
    high = dft.astype(jnp.bfloat16)
    low = (dft - high.astype(np.float32)).astype(jnp.bfloat16)
    return np.concatenate([high, low], axis=0)


def nt_dot(left, right):
    return lax.dot_general(
        left, right, (((1,), (1,)), ((), ())), preferred_element_type=jnp.float32
    )


def whiten_kernel(raw_ref, dft_ref, out_ref, chunk_ref, table_ref, balanced_ref, white_ref, sems):
    rows = CHUNK * 8
    copies = [
        pltpu.make_async_copy(
            raw_ref.at[pl.ds(chunk * rows, rows)], chunk_ref.at[chunk], sems.at[chunk]
        )
        for chunk in range(CHUNKS)
    ]
    for copy in copies:
        copy.start()
    table_copy = pltpu.make_async_copy(dft_ref, table_ref, sems.at[CHUNKS])
    table_copy.start()
    here = lax.broadcasted_iota(jnp.int32, (SAMPLES, SAMPLES), 0)
    there = lax.broadcasted_iota(jnp.int32, (SAMPLES, SAMPLES), 1)
    near = jnp.abs(here - there) <= SPAN // 2
    band = jnp.where(near, 1.0, 0.0).astype(jnp.bfloat16)
    per_half = CHUNKS // 2
    for half in range(2):
        for part in range(per_half):
            chunk = half * per_half + part
            copies[chunk].wait()
            flat = chunk_ref[chunk]
            total = jnp.dot(jnp.abs(flat), band, preferred_element_type=jnp.float32)
            balanced = flat.astype(jnp.float32) / (total * (1.0 / SPAN) + 1e-06)
            for lane in range(4):
                balanced_ref[lane, pl.ds(chunk * rows, rows), :] = balanced[
                    :, lane * 128 : (lane + 1) * 128
                ]
        if half == 0:
            table_copy.wait()
            dft = table_ref[...]
        first = half * HALF * 8
        for channel in range(8):
            balanced = jnp.concatenate(
                [
                    balanced_ref[lane, pl.ds(first + channel, HALF, stride=8), :]
                    for lane in range(4)
                ],
                axis=1,
            )
            high = balanced.astype(jnp.bfloat16)
            low = (balanced - high.astype(jnp.float32)).astype(jnp.bfloat16)
            wide = nt_dot(dft, high)
            spectrum = wide[: 2 * BINS] + (wide[2 * BINS :] + nt_dot(dft[: 2 * BINS], low))
            real = spectrum[:BINS]
            imag = spectrum[BINS:]
            energy = real * real + imag * imag
            level = jnp.mean(energy, axis=0, keepdims=True)
            factor = lax.rsqrt(energy + 0.25 * level + 1.0)
            at = half * HALF
            white_ref[:, channel, at : at + HALF] = real * factor
            white_ref[:, channel, WINDOWS + at : WINDOWS + at + HALF] = imag * factor
    out_ref[...] = white_ref[...].astype(jnp.bfloat16)


def whiten(raw):
    anywhere = pl.BlockSpec(memory_space=pl.ANY)
    return pl.pallas_call(
        whiten_kernel,
        in_specs=[anywhere, anywhere],
        out_specs=pl.BlockSpec(memory_space=pltpu.VMEM),
        out_shape=jax.ShapeDtypeStruct((BINS, 8, 2 * WINDOWS), jnp.bfloat16),
        scratch_shapes=[
            pltpu.VMEM((CHUNKS, CHUNK * 8, SAMPLES), jnp.bfloat16),
            pltpu.VMEM((4 * BINS, SAMPLES), jnp.bfloat16),
            pltpu.VMEM((4, WINDOWS * 8, 128), jnp.float32),
            pltpu.VMEM((BINS, 8, 2 * WINDOWS), jnp.float32),
            pltpu.SemaphoreType.DMA((CHUNKS + 1,)),
        ],
        compiler_params=pltpu.CompilerParams(vmem_limit_bytes=60 << 20),
        cost_estimate=pl.CostEstimate(
            flops=3_000_000_000, bytes_accessed=3 << 20, transcendentals=1 << 20
        ),
        name="whiten",
    )(raw.reshape(WINDOWS * 8, SAMPLES), jnp.asarray(dft_table()))


def multiply(left, right):
    turned = jnp.concatenate([left[:, WINDOWS:], -left[:, :WINDOWS]], axis=1)
    both = jnp.concatenate([left, turned], axis=0)
    tile = (nt_dot(both, right) * (1.0 / WINDOWS)).astype(jnp.bfloat16)
    return tile[:128], tile[128:]


def cross_kernel(place_ref, *refs):
    count = len(refs) - 4
    pieces = refs[:count]
    out_ref, right_ref, tile_ref, out_sem = refs[count:]

    def gather(b):
        for k, piece in enumerate(pieces[1:]):
            right_ref[b, place_ref[4 + k]] = piece[:, b]

    gather(0)
    outs = []
    for b in range(BINS):
        if b + 1 < BINS:
            gather(b + 1)
        left = pieces[0][:, b].reshape(128, 2 * WINDOWS)
        right = right_ref[b].reshape(256, 2 * WINDOWS)
        tile_ref[0, b], tile_ref[1, b] = multiply(left, right)
        if b % GROUP == GROUP - 1:
            bins = pl.ds(b - GROUP + 1, GROUP)
            copy = pltpu.make_async_copy(
                tile_ref.at[:, bins], out_ref.at[:, bins], out_sem.at[b // GROUP]
            )
            copy.start()
            outs.append(copy)
    for copy in outs:
        copy.wait()


def cross(places, pieces):
    out = (2, BINS, 128, 256)
    return pl.pallas_call(
        cross_kernel,
        in_specs=[pl.BlockSpec(memory_space=pltpu.SMEM)]
        + [pl.BlockSpec(memory_space=pltpu.VMEM)] * len(pieces),
        out_specs=pl.BlockSpec(memory_space=pl.ANY),
        out_shape=jax.ShapeDtypeStruct(out, jnp.bfloat16),
        scratch_shapes=[
            pltpu.VMEM((BINS, 8, 4, 8, 2 * WINDOWS), jnp.bfloat16),
            pltpu.VMEM(out, jnp.bfloat16),
            pltpu.SemaphoreType.DMA((BINS // GROUP,)),
        ],
        compiler_params=pltpu.CompilerParams(vmem_limit_bytes=20 << 20),
        cost_estimate=pl.CostEstimate(
            flops=1_100_000_000, bytes_accessed=8 << 20, transcendentals=0
        ),
        name="cross",
    )(places, *pieces)


def flat(z, yh, core, x, yl):
    return (((z * 2 + yh) * 2 + core) * 4 + x) * 4 + yl


def everyone():
    for index in np.ndindex(*(SIZES[a] for a in AXES)):
        yield index


def layer_class(z, x):
    return (x + z + z // 2) % 4


def ring_distance(a, b):
    return min((a - b) % 8, (b - a) % 8)


def spread_pairs():
    pairs = []
    for z, yh, x in np.ndindex(8, 2, 4):
        home = z * 2 + yh
        layer = layer_class(z, x)
        wanted = [(layer + 4 * up, half) for up in range(2) for half in range(2)]

        def way(order):
            return sum(
                ring_distance(4 * yh + yl, 4 * half + home % 4)
                for yl, (_, half) in enumerate(order)
            )

        order = min(itertools.permutations(wanted), key=way)
        for yl, (to_z, half) in enumerate(order):
            for core in range(2):
                pairs.append(
                    (flat(z, yh, core, x, yl), flat(to_z, half, core, home // 4, home % 4))
                )
    return pairs


def ring(value, axis, by):
    n = SIZES[axis]
    return lax.ppermute(value, axis, [(i, (i + by) % n) for i in range(n)])


def swap(value):
    return ring(value, "core", 1)


def places_here():
    table = []
    for z, yh, core, x, yl in everyone():
        rows = [(x + away) % 4 for away in (0, -1, 1, 2)]
        cols = []
        home_z = (x * 4 + yl) // 2
        for side in (core, 1 - core):
            for away in (0, -1, 1, 2):
                layer = (z + away) % 8
                (from_x,) = (k for k in range(4) if layer_class(home_z, k) == layer % 4)
                cols.append(side * 4 + from_x)
        assert sorted(rows) == list(range(4)) and sorted(cols) == list(range(8))
        table.append(rows + cols)
    table = jnp.asarray(np.array(table, np.int32))
    return lax.dynamic_index_in_dim(table, lax.axis_index(AXES), keepdims=False)


def on_device(raw):
    white = whiten(raw)
    near = lax.all_gather(white, "yl")
    here = lax.ppermute(near, AXES, spread_pairs())
    rows = lax.all_to_all(jnp.broadcast_to(near[None], (4,) + near.shape), "x", 0, 0)
    rows = [rows.reshape((16,) + white.shape)]
    below = ring(here, "z", 1)
    above = ring(here, "z", -1)
    far = jnp.concatenate([ring(below[:2], "z", 1), ring(above[2:], "z", -1)])
    mine = [here, below, above, far]
    pieces = rows + mine + [swap(piece) for piece in mine]
    return cross(places_here(), pieces)


def solution(mesh):
    split = Mesh(mesh.devices.reshape([SIZES[a] for a in AXES]), AXES)
    return jax.shard_map(
        on_device,
        mesh=split,
        in_specs=(P(None, AXES, None),),
        out_specs=P(None, None, ("z", "yh", "core"), ("x", "yl")),
        check_vma=False,
    )
```
